256 devices in a mesh: fsdp: 64 (over x, z, core), grp: 4 (over y).
Axes of the slice: x: 4, y: 4, z: 8, core: 2. Of those that a mesh axis runs over, the one named last changes fastest.
Arguments:
- right_factor: bfloat16 [64, 1024, 1024], P(None, 'fsdp', 'grp')
- left_factor: bfloat16 [64, 512, 512], P(None, 'fsdp', 'grp')
- right_basis: float32 [64, 1024, 1024], P(None, 'fsdp', 'grp')
- left_basis: float32 [64, 512, 512], P(None, 'fsdp', 'grp')
- moment: bfloat16 [64, 512, 1024], P(None, 'fsdp', 'grp'), may hold values from -6 to 6
- owner: int32 [64], replicated, may hold values from 0 to 63, as said below
- row_extent: int32 [64], replicated, may hold values from 256 to 512
- col_extent: int32 [64], replicated, may hold values from 512 to 1024
Outputs:
- right_refreshed: float32 [64, 2, 1024, 1024], P('fsdp', None, None, 'grp')
- left_refreshed: float32 [64, 2, 512, 512], P('fsdp', None, None, 'grp')
- new_moment: bfloat16 [64, 512, 1024], P(None, 'fsdp', 'grp')
The draws below stay inside these ranges and needn't reach their ends.
Inputs may be any that keep to these rules, and one draw needn't show every extreme that they name: At most 2 blocks share an owner; in every draw some owner holds exactly 2 blocks and some owners hold none.
All inputs are finite; a program needn't handle non-finite values.
Results may differ from the reference program's by a relative error of at most 0.0085.
Values may be sent and summed in bfloat16 or wider, within the bound.
No kernel may reach another device: no remote copies, remote signals or barrier semaphores. Data moves between devices by JAX's collectives and lax.ppermute only.
A program may use at most 128 MiB of HBM per device.

```python
import math
import jax
import jax.numpy as jnp
from jax import lax

BL = 512
BR = 1024
MOST = 2
NBLK = 64
N_FSDP = 64


def positive_factor(noise_draw, factor_key, order_size):
    diagonal_key, spike_key, strength_key = jax.random.split(factor_key, 3)
    off_diag = (noise_draw + jnp.swapaxes(noise_draw, 1, 2)) * (0.5 / math.sqrt(2.0 * order_size))
    diagonal = jax.random.uniform(diagonal_key, noise_draw.shape[:2], jnp.float32, 1.5, 3.0)
    direction = jax.random.normal(spike_key, noise_draw.shape[:2], jnp.float32) * (1.0 / math.sqrt(order_size))
    strength = jax.random.uniform(strength_key, noise_draw.shape[:1], jnp.float32, 8.0, 16.0)
    spike_term = strength[:, None, None] * direction[:, :, None] * direction[:, None, :]
    return off_diag + diagonal[:, :, None] * jnp.eye(order_size, dtype=jnp.float32)[None] + spike_term


def stale_basis(noise_draw, order_size):
    return jnp.eye(order_size, dtype=jnp.float32)[None] + noise_draw * (0.3 / math.sqrt(order_size))


def extent_draw(key, low_value, high_value):
    value_key, top_key, bottom_key = jax.random.split(key, 3)
    values = jax.random.randint(value_key, (NBLK,), low_value, high_value + 1)
    top_pick = jax.random.randint(top_key, (), 0, NBLK)
    low_pick = (top_pick + 1 + jax.random.randint(bottom_key, (), 0, NBLK - 1)) % NBLK
    block_ids = jnp.arange(NBLK, dtype=jnp.int32)
    values = jnp.where(block_ids == top_pick, high_value, values)
    return jnp.where(block_ids == low_pick, low_value, values).astype(jnp.int32)


def draw_right_factor(key, part):
    key = jax.random.fold_in(key, 11)
    noise_key, factor_key = jax.random.split(key)
    noise_draw = jax.random.normal(noise_key, (NBLK, BR, BR), jnp.float32)
    return positive_factor(noise_draw, factor_key, BR).astype(jnp.bfloat16)


def draw_left_factor(key, part):
    key = jax.random.fold_in(key, 13)
    noise_key, factor_key = jax.random.split(key)
    noise_draw = jax.random.normal(noise_key, (NBLK, BL, BL), jnp.float32)
    return positive_factor(noise_draw, factor_key, BL).astype(jnp.bfloat16)


def draw_right_basis(key, part):
    key = jax.random.fold_in(key, 17)
    noise_draw = jax.random.normal(key, (NBLK, BR, BR), jnp.float32)
    return stale_basis(noise_draw, BR)


def draw_left_basis(key, part):
    key = jax.random.fold_in(key, 19)
    noise_draw = jax.random.normal(key, (NBLK, BL, BL), jnp.float32)
    return stale_basis(noise_draw, BL)


def draw_owner(key, part):
    key = jax.random.fold_in(key, 31)
    mix_key, place_key = jax.random.split(key)
    inner_ids = (jax.random.permutation(mix_key, NBLK - 2) + 1).astype(jnp.int32)
    double_count = NBLK // 4
    ends = jnp.array([0, NBLK - 1], dtype=jnp.int32)
    listed = jnp.concatenate([ends, inner_ids[:double_count], inner_ids[:NBLK - 2 - double_count]])
    placement = jax.random.permutation(place_key, NBLK)
    return jnp.zeros((NBLK,), jnp.int32).at[placement].set(listed)


def draw_row_extent(key, part):
    key = jax.random.fold_in(key, 41)
    return extent_draw(key, BL // 2, BL)


def draw_col_extent(key, part):
    key = jax.random.fold_in(key, 43)
    return extent_draw(key, BR // 2, BR)


def level_of(key, shape, cuts, least, high):
    gain, own = 1.0, jax.random.fold_in(key, 6)
    for position, shards_of in cuts:
        draws = jnp.exp(jax.random.uniform(jax.random.fold_in(own, position), (shards_of,), jnp.float32, least / len(cuts), high / len(cuts)))
        gain = gain * jnp.repeat(draws, shape[position] // shards_of).reshape([-1 if axis == position else 1 for axis in range(len(shape))])
    return gain


def noise(rng, dims, scale, most, cuts=(), held_as=jnp.bfloat16):
    entries = scale * jax.random.normal(rng, dims, jnp.float32)
    if cuts:
        entries = entries * level_of(rng, dims, cuts, -0.22, 0.18)
    return jnp.clip(entries, -most, most).astype(held_as)


def setup_inputs(seed: int = 0) -> dict:
    seeds = jax.random.split(jax.random.key(seed), 9)
    right_factor = draw_right_factor(jax.random.fold_in(seeds[8], 71), 0)
    left_factor = draw_left_factor(jax.random.fold_in(seeds[8], 71), 0)
    right_basis = draw_right_basis(jax.random.fold_in(seeds[8], 71), 0)
    left_basis = draw_left_basis(jax.random.fold_in(seeds[8], 71), 0)
    moment = noise(seeds[4], (NBLK, BL, BR), 1.0, 6.0, ((1, 64), (2, 4)))
    owner = draw_owner(jax.random.fold_in(seeds[8], 71), 0)
    row_extent = draw_row_extent(jax.random.fold_in(seeds[8], 71), 0)
    col_extent = draw_col_extent(jax.random.fold_in(seeds[8], 71), 0)
    return dict(right_factor=right_factor, left_factor=left_factor, right_basis=right_basis, left_basis=left_basis, moment=moment, owner=owner, row_extent=row_extent, col_extent=col_extent)


def masked(factor, extent):
    width_ids = jnp.arange(factor.shape[0], dtype=jnp.int32)
    inside = (width_ids[:, None] < extent) & (width_ids[None, :] < extent)
    unit = (width_ids[:, None] == width_ids[None, :]).astype(factor.dtype)
    return jnp.where(inside, factor, unit)

def orthonormal(power_cols):
    contract = (((0,), (0,)), ((), ()))
    gram_matrix = lax.dot_general(power_cols.astype(jnp.float32), power_cols.astype(jnp.float32), contract, preferred_element_type=jnp.float32)
    lower_factor = jnp.linalg.cholesky(gram_matrix)
    unit = jnp.eye(gram_matrix.shape[0], dtype=jnp.float32)
    lower_inverse = jax.scipy.linalg.solve_triangular(lower_factor, unit, lower=True)
    return jnp.dot(power_cols.astype(jnp.float32), lower_inverse.T.astype(jnp.float32), precision=lax.Precision.HIGHEST, preferred_element_type=jnp.float32)

def refresh_block(block_items):
    right_slice, left_slice, right_old, left_old, moment_block, row_limit, col_limit = block_items
    basis_r = right_old.astype(jnp.bfloat16)
    basis_l = left_old.astype(jnp.bfloat16)
    power_r = jnp.dot(masked(right_slice, col_limit).astype(jnp.float32), basis_r.astype(jnp.float32), preferred_element_type=jnp.float32).astype(jnp.bfloat16)
    power_l = jnp.dot(masked(left_slice, row_limit).astype(jnp.float32), basis_l.astype(jnp.float32), preferred_element_type=jnp.float32).astype(jnp.bfloat16)
    fresh_r = orthonormal(power_r)
    fresh_l = orthonormal(power_l)
    carried = lax.dot_general(moment_block.astype(jnp.float32), basis_r.astype(jnp.float32), (((1,), (1,)), ((), ())), preferred_element_type=jnp.float32)
    turned = jnp.dot(carried.astype(jnp.bfloat16).astype(jnp.float32), fresh_r.astype(jnp.bfloat16).astype(jnp.float32), preferred_element_type=jnp.float32).astype(jnp.bfloat16)
    left_mixer = lax.dot_general(fresh_l.astype(jnp.bfloat16).astype(jnp.float32), basis_l.astype(jnp.float32), (((0,), (0,)), ((), ())), preferred_element_type=jnp.float32).astype(jnp.bfloat16)
    rotated = jnp.dot(left_mixer.astype(jnp.float32), turned.astype(jnp.float32), preferred_element_type=jnp.float32).astype(jnp.bfloat16)
    return (fresh_r, fresh_l, rotated)

def reference(right_factor, left_factor, right_basis, left_basis, moment, owner, row_extent, col_extent):
    fresh_r, fresh_l, new_moment = lax.map(refresh_block, (right_factor, left_factor, right_basis, left_basis, moment, row_extent, col_extent))
    block_ids = jnp.arange(owner.shape[0], dtype=jnp.int32)
    same_owner = owner[:, None] == owner[None, :]
    owner_rank = jnp.sum((same_owner & (block_ids[None, :] < block_ids[:, None])).astype(jnp.int32), axis=1)
    slot_ids = owner * MOST + owner_rank
    slot_total = N_FSDP * MOST
    right_out = jnp.broadcast_to(jnp.eye(BR, dtype=jnp.float32), (slot_total, BR, BR)).at[slot_ids].set(fresh_r)
    left_out = jnp.broadcast_to(jnp.eye(BL, dtype=jnp.float32), (slot_total, BL, BL)).at[slot_ids].set(fresh_l)
    return (right_out.reshape(N_FSDP, MOST, BR, BR), left_out.reshape(N_FSDP, MOST, BL, BL), new_moment)
```

```python
import jax
import jax.numpy as jnp
from jax import lax
from jax.experimental import pallas as pl
from jax.experimental.pallas import tpu as pltpu
from jax.sharding import PartitionSpec as P

MOST = 2
TILE = 128
SLAB = 8
HIGHEST = lax.Precision.HIGHEST
BF16 = jnp.bfloat16
F32 = jnp.float32


def lane_copy(tile, lane):
    return jnp.broadcast_to(tile[:, lane : lane + 1], (SLAB, TILE))


def row_copy(tile, row):
    return jnp.broadcast_to(tile[row : row + 1, :], (SLAB, TILE))


def tile_inverse(rows):
    lane = lax.broadcasted_iota(jnp.int32, (SLAB, TILE), 1)
    sub = lax.broadcasted_iota(jnp.int32, (SLAB, TILE), 0)
    rows = list(rows)
    count = len(rows)
    for s in range(count):
        start = SLAB * s
        inside = (lane >= start) & (lane < start + SLAB)
        columns = [lane_copy(rows[s], start + c) for c in range(SLAB)]
        forward = jnp.where(inside, (lane - start == sub).astype(F32), rows[s])
        full = forward
        pivots = jnp.ones((SLAB, TILE), F32)
        for k in range(SLAB):
            pivot = row_copy(columns[k], k)
            scaled = columns[k] * (1.0 / pivot)
            below = jnp.where(sub > k, scaled, 0.0)
            others = jnp.where(sub != k, scaled, 0.0)
            for c in range(k + 1, SLAB):
                columns[c] = columns[c] - others * row_copy(columns[c], k)
            if k < SLAB - 1:
                forward = forward - below * row_copy(forward, k)
            full = full - others * row_copy(full, k)
            pivots = jnp.where(sub == k, pivot, pivots)
        rows[s] = forward * lax.rsqrt(pivots)
        if s + 1 < count:
            full = full * (1.0 / pivots)
            spread = [row_copy(full, j) for j in range(SLAB)]
        for i in range(s + 1, count):
            total = jnp.where(inside, 0.0, rows[i])
            for j in range(SLAB):
                total = total - lane_copy(rows[i], start + j) * spread[j]
            rows[i] = total
    return [jnp.where(lane <= sub + SLAB * s, rows[s], 0.0) for s in range(count)]


def dot32(a, b, dims=((1,), (0,))):
    return lax.dot_general(a, b, (dims, ((), ())), precision=HIGHEST, preferred_element_type=F32)


def inverse_kernel(gram_ref, out_ref, tile_ref):
    order = out_ref.shape[0]
    steps = order // TILE
    out_ref[...] = gram_ref[...]

    def step(k, carry):
        block = pl.ds(pl.multiple_of(k * TILE, TILE), TILE)
        tile_ref[...] = out_ref[block, block]
        slabs = [tile_ref[SLAB * i : SLAB * (i + 1), :] for i in range(TILE // SLAB)]
        for i, slab in enumerate(tile_inverse(slabs)):
            tile_ref[SLAB * i : SLAB * (i + 1), :] = slab
        for j in range(steps):

            @pl.when(k == j)
            def _():
                own = slice(j * TILE, (j + 1) * TILE)
                rest = slice((j + 1) * TILE, order)
                left = order - (j + 1) * TILE
                inverse = tile_ref[...]
                out_ref[own, :] = dot32(inverse, out_ref[own, :])
                out_ref[own, own] = inverse
                if left:
                    lower = dot32(out_ref[rest, own], inverse, ((1,), (1,)))
                    out_ref[rest, own] = jnp.zeros((left, TILE), F32)
                    out_ref[rest, :] -= dot32(lower, out_ref[own, :])
                    out_ref[own, rest] = jnp.zeros((TILE, left), F32)

        return carry

    lax.fori_loop(0, steps, step, 0)


def lower_inverse(gram):
    order = gram.shape[0]
    return pl.pallas_call(
        inverse_kernel,
        out_shape=jax.ShapeDtypeStruct((order, order), F32),
        in_specs=[pl.BlockSpec(memory_space=pltpu.VMEM)],
        out_specs=pl.BlockSpec(memory_space=pltpu.VMEM),
        scratch_shapes=[pltpu.VMEM((TILE, TILE), F32)],
        compiler_params=pltpu.CompilerParams(vmem_limit_bytes=32 * 2**20),
        cost_estimate=pl.CostEstimate(
            flops=20 * order**3, bytes_accessed=8 * order**2, transcendentals=0
        ),
        name="lower_inverse",
    )(gram)


def eye_piece(row_count, col_count, col_start):
    row_ids = lax.broadcasted_iota(jnp.int32, (row_count, col_count), 0)
    col_ids = lax.broadcasted_iota(jnp.int32, (row_count, col_count), 1) + col_start
    return (row_ids == col_ids).astype(F32)


def masked_factor(local_shard, extent, row_start, col_start):
    grid_shape = local_shard.shape
    row_ids = lax.broadcasted_iota(jnp.int32, grid_shape, 1) + row_start
    col_ids = lax.broadcasted_iota(jnp.int32, grid_shape, 2) + col_start
    extent_grid = extent[:, None, None]
    inside = (row_ids < extent_grid) & (col_ids < extent_grid)
    return jnp.where(inside, local_shard, (row_ids == col_ids).astype(local_shard.dtype))


def slot_tables(owner, owner_count):
    block_count = owner.shape[0]
    block_ids = jnp.arange(block_count, dtype=jnp.int32)
    same_owner = owner[:, None] == owner[None, :]
    owner_rank = jnp.sum(
        (same_owner & (block_ids[None, :] < block_ids[:, None])).astype(jnp.int32), axis=1
    )
    slot_ids = owner * MOST + owner_rank
    slot_hits = slot_ids[:, None] == jnp.arange(owner_count * MOST, dtype=jnp.int32)[None, :]
    block_of = jnp.sum(jnp.where(slot_hits, block_ids[:, None], 0), axis=0)
    filled = jnp.any(slot_hits, axis=0)
    return (block_of, filled)


def swap(pieces):
    return lax.all_to_all(pieces, "fsdp", split_axis=0, concat_axis=0, tiled=True)


def dot(a, b, dims=((1,), (0,))):
    return lax.dot_general(a, b, (dims, ((), ())), preferred_element_type=F32)


def fresh_columns(power, inverse_rows):
    high = inverse_rows.astype(BF16)
    low = (inverse_rows - high.astype(F32)).astype(BF16)
    across = ((1,), (1,))
    return (dot(power, high, across) + dot(power, low, across)).astype(BF16)


def to_slots(rows_of_blocks, block_of, owner_count):
    picked = jnp.take(rows_of_blocks, block_of, axis=0)
    picked = picked.reshape((owner_count, MOST) + rows_of_blocks.shape[1:])
    return lax.all_to_all(picked, "fsdp", split_axis=0, concat_axis=2, tiled=True)[0]


def per_device(
    right_factor, left_factor, right_basis, left_basis, moment, owner, row_extent, col_extent
):
    owner_count = lax.axis_size("fsdp")
    fsdp_index = lax.axis_index("fsdp")
    group_index = lax.axis_index("grp")
    right_rows, right_cols = right_factor.shape[1:]
    left_rows, left_cols = left_factor.shape[1:]
    order_r = right_rows * owner_count
    order_l = left_rows * owner_count
    block_of, filled = slot_tables(owner, owner_count)
    right_masked = masked_factor(
        right_factor, col_extent, fsdp_index * right_rows, group_index * right_cols
    )
    left_masked = masked_factor(
        left_factor, row_extent, fsdp_index * left_rows, group_index * left_cols
    )
    left_pack = jnp.concatenate(
        [moment, jnp.concatenate([left_masked, left_basis.astype(BF16)], axis=2)], axis=1
    )
    factor_r = swap(right_masked).reshape(order_r, right_cols)
    basis_r = swap(right_basis.astype(BF16)).reshape(order_r, right_cols)
    left_pack = swap(left_pack)
    moment_in = left_pack[:, :left_rows].reshape(order_l, right_cols)
    left_pair = left_pack[:, left_rows:].reshape(order_l, 2 * left_cols)
    factor_r = lax.all_gather(factor_r, "grp", axis=1, tiled=True)
    basis_r = lax.all_gather(basis_r, "grp", axis=1, tiled=True)
    moment_in = lax.all_gather(moment_in, "grp", axis=1, tiled=True)
    left_pair = lax.all_gather(left_pair, "grp", axis=0)
    factor_l, basis_l = (
        jnp.concatenate([left_pair[g, :, a : a + left_cols] for g in range(left_pair.shape[0])], 1)
        for a in (0, left_cols)
    )

    power_r = dot(factor_r, basis_r).astype(BF16)
    inverse_r = lower_inverse(dot(power_r, power_r, ((0,), (0,))))
    fresh_r = fresh_columns(
        power_r, lax.dynamic_slice_in_dim(inverse_r, group_index * right_cols, right_cols, 0)
    )
    rows_r = swap(fresh_r.reshape(owner_count, right_rows, right_cols))

    power_l = dot(factor_l, basis_l).astype(BF16)
    inverse_l = lower_inverse(dot(power_l, power_l, ((0,), (0,))))
    fresh_l = fresh_columns(power_l, inverse_l)
    carried = dot(moment_in, basis_r, ((1,), (1,))).astype(BF16)
    turned = dot(carried, fresh_r).astype(BF16)
    left_mixer = dot(fresh_l, basis_l, ((0,), (0,))).astype(BF16)
    moment_out = dot(left_mixer, turned).astype(BF16)
    left_new = lax.dynamic_slice_in_dim(fresh_l, group_index * left_cols, left_cols, 1)
    back = jnp.concatenate([moment_out, left_new], axis=1)
    back = swap(back.reshape(owner_count, left_rows, right_cols + left_cols))
    new_moment = back[:, :, :right_cols]

    right_out = to_slots(rows_r, block_of, owner_count)
    left_out = to_slots(back[:, :, right_cols:], block_of, owner_count)
    mine = lax.dynamic_slice_in_dim(filled, fsdp_index * MOST, MOST)[:, None, None]
    right_out = jnp.where(
        mine, right_out.astype(F32), eye_piece(order_r, right_cols, group_index * right_cols)
    )
    left_out = jnp.where(
        mine, left_out.astype(F32), eye_piece(order_l, left_cols, group_index * left_cols)
    )
    return (right_out[None], left_out[None], new_moment)


def solution(mesh):
    return jax.shard_map(
        per_device,
        mesh=mesh,
        in_specs=(
            P(None, "fsdp", "grp"),
            P(None, "fsdp", "grp"),
            P(None, "fsdp", "grp"),
            P(None, "fsdp", "grp"),
            P(None, "fsdp", "grp"),
            P(),
            P(),
            P(),
        ),
        out_specs=(
            P("fsdp", None, None, "grp"),
            P("fsdp", None, None, "grp"),
            P(None, "fsdp", "grp"),
        ),
        check_vma=False,
    )
```

```python
import functools

import jax
import jax.numpy as jnp
from jax import lax
from jax.experimental import pallas as pl
from jax.experimental.pallas import tpu as pltpu
from jax.sharding import PartitionSpec as P

MOST = 2
TILE = 128
SLAB = 8
HIGHEST = lax.Precision.HIGHEST
BF16 = jnp.bfloat16
F32 = jnp.float32


def lane_copy(tile, lane):
    return jnp.broadcast_to(tile[:, lane : lane + 1], (SLAB, TILE))


def row_copy(tile, row):
    return jnp.broadcast_to(tile[row : row + 1, :], (SLAB, TILE))


def tile_inverse(rows):
    lane = lax.broadcasted_iota(jnp.int32, (SLAB, TILE), 1)
    sub = lax.broadcasted_iota(jnp.int32, (SLAB, TILE), 0)
    rows = list(rows)
    count = len(rows)
    for s in range(count):
        start = SLAB * s
        inside = (lane >= start) & (lane < start + SLAB)
        columns = [lane_copy(rows[s], start + c) for c in range(SLAB)]
        forward = jnp.where(inside, (lane - start == sub).astype(F32), rows[s])
        full = forward
        pivots = jnp.ones((SLAB, TILE), F32)
        for k in range(SLAB):
            pivot = row_copy(columns[k], k)
            others = jnp.where(sub != k, columns[k], 0.0)
            below = jnp.where(sub > k, columns[k], 0.0)
            products = [others * row_copy(columns[c], k) for c in range(k + 1, SLAB)]
            forward_part = below * row_copy(forward, k)
            full_part = others * row_copy(full, k)
            scale = 1.0 / pivot
            for c in range(k + 1, SLAB):
                columns[c] = columns[c] - products[c - k - 1] * scale
            forward = forward - forward_part * scale
            full = full - full_part * scale
            pivots = jnp.where(sub == k, pivot, pivots)
        rows[s] = forward * lax.rsqrt(pivots)
        if s + 1 < count:
            full = full * (1.0 / pivots)
            spread = [row_copy(full, j) for j in range(SLAB)]
        for i in range(s + 1, count):
            total = jnp.where(inside, 0.0, rows[i])
            for j in range(SLAB):
                total = total - lane_copy(rows[i], start + j) * spread[j]
            rows[i] = total
    return [jnp.where(lane <= sub + SLAB * s, rows[s], 0.0) for s in range(count)]


def dot32(a, b, dims=((1,), (0,))):
    return lax.dot_general(a, b, (dims, ((), ())), precision=HIGHEST, preferred_element_type=F32)


def dot(a, b, dims=((1,), (0,))):
    return lax.dot_general(a, b, (dims, ((), ())), preferred_element_type=F32)


def read_slabs(tile_ref):
    return [tile_ref[SLAB * i : SLAB * (i + 1), :] for i in range(TILE // SLAB)]


def write_slabs(tile_ref, slabs):
    for i, slab in enumerate(slabs):
        tile_ref[SLAB * i : SLAB * (i + 1), :] = slab


def invert(mat, tile, row, low):
    order = mat.shape[0]
    chunk = 256
    tile[...] = mat[:TILE, :TILE]
    write_slabs(tile, tile_inverse(read_slabs(tile)))
    lanes = lax.broadcasted_iota(jnp.int32, (TILE, order), 1)
    row_ids = lax.broadcasted_iota(jnp.int32, (order, TILE), 0)

    def step(k, carry):
        start = pl.multiple_of(k * TILE, TILE)
        after = pl.multiple_of(start + TILE, TILE)
        own = pl.ds(start, TILE)
        following = pl.ds(after, TILE)
        inverse = tile[...]
        row[...] = dot32(inverse, mat[own, :])
        row[:, own] = inverse
        column = mat[:, own]
        low[...] = jnp.where(row_ids >= after, dot32(column, inverse, ((1,), (1,))), 0.0)
        mat[:, own] = jnp.where(row_ids >= after, 0.0, column)
        mat[own, :] = jnp.where(lanes < after, row[...], 0.0)
        tile[...] = mat[following, following] - dot32(low[following, :], row[:, following])
        slabs = read_slabs(tile)
        for c in range(0, order, chunk):
            mat[:, c : c + chunk] -= dot32(low[...], row[:, c : c + chunk])
        write_slabs(tile, tile_inverse(slabs))
        return carry

    lax.fori_loop(0, order // TILE - 1, step, 0)
    last = order - TILE
    inverse = tile[...]
    mat[last:, :] = dot32(inverse, mat[last:, :])
    mat[last:, last:] = inverse


def split32(value):
    high = value.astype(BF16)
    return high, (value - high.astype(F32)).astype(BF16)


def basis_kernel(all_columns, first, own, following, previous, far_factor, far_basis, fresh, basis, factor, power, mat, tile, row, low):
    order = basis.shape[0]
    width = own.shape[1]
    group = first[0]
    top, bottom = slice(0, order), slice(order, 2 * order)
    for shift, piece in ((0, own), (1, following), (3, previous), (2, None)):
        columns = pl.ds(pl.multiple_of(lax.rem(group + shift, 4) * width, TILE), width)
        factor[:, columns] = far_factor[...] if piece is None else piece[top, :]
        basis[:, columns] = far_basis[...] if piece is None else piece[bottom, :]
    for c in range(0, order, width):
        power[:, c : c + width] = dot(factor[...], basis[:, c : c + width]).astype(BF16)
    for c in range(0, order, width):
        mat[:, c : c + width] = dot(power[...], power[:, c : c + width], ((0,), (0,)))
    invert(mat, tile, row, low)
    across = ((1,), (1,))
    if all_columns:
        for c in range(0, order, width):
            high, low_part = split32(mat[c : c + width, :])
            total = dot(power[...], high, across) + dot(power[...], low_part, across)
            fresh[:, c : c + width] = total.astype(BF16)
    else:
        high, low_part = split32(mat[pl.ds(pl.multiple_of(group * width, TILE), width), :])
        total = dot(power[...], high, across) + dot(power[...], low_part, across)
        fresh[...] = total.astype(BF16)


VMEM = pl.BlockSpec(memory_space=pltpu.VMEM)
SMEM = pl.BlockSpec(memory_space=pltpu.SMEM)


def fresh_basis(pieces, group_index, all_columns):
    order, width = pieces[3].shape
    return pl.pallas_call(
        functools.partial(basis_kernel, all_columns),
        out_shape=(
            jax.ShapeDtypeStruct((order, order if all_columns else width), BF16),
            jax.ShapeDtypeStruct((order, order), BF16),
        ),
        in_specs=[SMEM] + [VMEM] * 5,
        out_specs=(VMEM, VMEM),
        scratch_shapes=[
            pltpu.VMEM((order, order), BF16),
            pltpu.VMEM((order, order), BF16),
            pltpu.VMEM((order, order), F32),
            pltpu.VMEM((TILE, TILE), F32),
            pltpu.VMEM((TILE, order), F32),
            pltpu.VMEM((order, TILE), F32),
        ],
        compiler_params=pltpu.CompilerParams(vmem_limit_bytes=40 * 2**20),
        cost_estimate=pl.CostEstimate(
            flops=6 * 10**7 * order, bytes_accessed=10 * order**2, transcendentals=0
        ),
        name="fresh_basis_all" if all_columns else "fresh_basis_own",
    )(group_index, *pieces)


def rotate_kernel(first, own, following, previous, far_top, far_bottom, basis_r, fresh_r, fresh_l, basis_l, out, moment):
    width = own.shape[1]
    half = own.shape[0] // 2
    for shift, piece in ((0, own), (1, following), (3, previous), (2, None)):
        columns = pl.ds(pl.multiple_of(lax.rem(first[0] + shift, 4) * width, TILE), width)
        if piece is None:
            moment[:half, columns] = far_top[...]
            moment[half:, columns] = far_bottom[...]
        else:
            moment[:, columns] = piece[...]
    carried = dot(moment[...], basis_r[...], ((1,), (1,))).astype(BF16)
    turned = dot(carried, fresh_r[...]).astype(BF16)
    mixer = dot(fresh_l[...], basis_l[...], ((0,), (0,))).astype(BF16)
    out[...] = dot(mixer, turned).astype(BF16)


def rotate(pieces, group_index, basis_r, fresh_r, fresh_l, basis_l):
    rows, width = pieces[0].shape
    return pl.pallas_call(
        rotate_kernel,
        out_shape=jax.ShapeDtypeStruct((rows, width), BF16),
        in_specs=[SMEM] + [VMEM] * 9,
        out_specs=VMEM,
        scratch_shapes=[pltpu.VMEM((rows, basis_r.shape[0]), BF16)],
        compiler_params=pltpu.CompilerParams(vmem_limit_bytes=24 * 2**20),
        cost_estimate=pl.CostEstimate(flops=2 * 10**9, bytes_accessed=6 * 2**20, transcendentals=0),
        name="rotate",
    )(group_index, *pieces, basis_r, fresh_r, fresh_l, basis_l)


def shifted(piece, shift):
    count = lax.axis_size("grp")
    return lax.ppermute(piece, "grp", [(i, (i + shift) % count) for i in range(count)])


def near(piece):
    return shifted(piece, 1), shifted(piece, -1)


def gathered(piece, previous, following):
    half = piece.shape[0] // 2
    return piece, following, previous, shifted(previous[:half], 1), shifted(following[half:], -1)


def gathered_at_once(piece):
    half = piece.shape[0] // 2
    return (
        piece,
        shifted(piece, -1),
        shifted(piece, 1),
        shifted(piece[:half], 2),
        shifted(piece[half:], -2),
    )


def eye_piece(row_count, col_count, col_start):
    row_ids = lax.broadcasted_iota(jnp.int32, (row_count, col_count), 0)
    col_ids = lax.broadcasted_iota(jnp.int32, (row_count, col_count), 1) + col_start
    return (row_ids == col_ids).astype(F32)


def masked_factor(local_shard, extent, row_start, col_start):
    grid_shape = local_shard.shape
    row_ids = lax.broadcasted_iota(jnp.int32, grid_shape, 1) + row_start
    col_ids = lax.broadcasted_iota(jnp.int32, grid_shape, 2) + col_start
    extent_grid = extent[:, None, None]
    inside = (row_ids < extent_grid) & (col_ids < extent_grid)
    return jnp.where(inside, local_shard, (row_ids == col_ids).astype(local_shard.dtype))


def slot_tables(owner, owner_count):
    block_count = owner.shape[0]
    block_ids = jnp.arange(block_count, dtype=jnp.int32)
    same_owner = owner[:, None] == owner[None, :]
    owner_rank = jnp.sum(
        (same_owner & (block_ids[None, :] < block_ids[:, None])).astype(jnp.int32), axis=1
    )
    slot_ids = owner * MOST + owner_rank
    slot_hits = slot_ids[:, None] == jnp.arange(owner_count * MOST, dtype=jnp.int32)[None, :]
    block_of = jnp.sum(jnp.where(slot_hits, block_ids[:, None], 0), axis=0)
    filled = jnp.any(slot_hits, axis=0)
    return (block_of, filled)


def swap(pieces):
    return lax.all_to_all(pieces, "fsdp", split_axis=0, concat_axis=0, tiled=True)


def per_device(
    right_factor, left_factor, right_basis, left_basis, moment, owner, row_extent, col_extent
):
    owner_count = lax.axis_size("fsdp")
    fsdp_index = lax.axis_index("fsdp")
    group_index = lax.axis_index("grp")
    right_rows, right_cols = right_factor.shape[1:]
    left_rows, left_cols = left_factor.shape[1:]
    order_r = right_rows * owner_count
    order_l = left_rows * owner_count
    block_of, filled = slot_tables(owner, owner_count)
    right_masked = masked_factor(
        right_factor, col_extent, fsdp_index * right_rows, group_index * right_cols
    )
    left_masked = masked_factor(
        left_factor, row_extent, fsdp_index * left_rows, group_index * left_cols
    )
    pack = jnp.concatenate(
        [
            right_masked,
            right_basis.astype(BF16),
            jnp.concatenate([left_masked, left_basis.astype(BF16)], axis=2),
            moment,
        ],
        axis=1,
    )
    pack = swap(pack)
    bounds = (0, right_rows, 2 * right_rows, 2 * right_rows + left_rows, 2 * (right_rows + left_rows))
    factor_r, basis_r, left_pair, moment_in = (
        pack[:, start:stop].reshape(-1, right_cols) for start, stop in zip(bounds, bounds[1:])
    )
    left_piece = jnp.concatenate([left_pair[:, :left_cols], left_pair[:, left_cols:]], axis=0)
    right_piece = jnp.concatenate([factor_r, basis_r], axis=0)
    group = group_index.astype(jnp.int32)[None]

    left_pieces = gathered(left_piece, *near(left_piece))
    left_pieces, right_piece = lax.optimization_barrier((left_pieces, right_piece))
    right_near = near(right_piece)
    fresh_l, basis_l = fresh_basis(left_pieces, group, True)
    fresh_l, right_near = lax.optimization_barrier((fresh_l, right_near))
    left_new = lax.dynamic_slice_in_dim(fresh_l, group_index * left_cols, left_cols, 1)
    rows_l = swap(left_new.reshape(owner_count, left_rows, left_cols))
    right_pieces = gathered(right_piece, *right_near)
    right_pieces, moment_in = lax.optimization_barrier((right_pieces, moment_in))
    moment_pieces = gathered_at_once(moment_in)
    fresh_r, basis_r = fresh_basis(right_pieces, group, False)
    moment_out = rotate(moment_pieces, group, basis_r, fresh_r, fresh_l, basis_l)
    back = jnp.concatenate(
        [
            fresh_r.reshape(owner_count, right_rows, right_cols),
            moment_out.reshape(owner_count, left_rows, right_cols),
        ],
        axis=1,
    )
    back = swap(back)
    new_moment = back[:, right_rows:]

    def to_slots(rows, slot):
        return jnp.take(rows, block_of[slot::MOST], axis=0, mode="clip")

    pair_l = jnp.concatenate([to_slots(rows_l, slot) for slot in range(MOST)], axis=2)
    slots = [to_slots(back[:, :right_rows], slot) for slot in range(MOST)]
    slots = swap(jnp.concatenate(slots + [pair_l], axis=1))
    right_out = jnp.stack(
        [
            slots[:, slot * right_rows : (slot + 1) * right_rows].reshape(order_r, right_cols)
            for slot in range(MOST)
        ]
    )
    pair_l = slots[:, MOST * right_rows :].reshape(order_l, MOST * left_cols)
    left_out = jnp.stack(
        [pair_l[:, slot * left_cols : (slot + 1) * left_cols] for slot in range(MOST)]
    )
    mine = lax.dynamic_slice_in_dim(filled, fsdp_index * MOST, MOST)[:, None, None]
    right_out = jnp.where(
        mine, right_out.astype(F32), eye_piece(order_r, right_cols, group_index * right_cols)
    )
    left_out = jnp.where(
        mine, left_out.astype(F32), eye_piece(order_l, left_cols, group_index * left_cols)
    )
    return (right_out[None], left_out[None], new_moment)


def solution(mesh):
    return jax.shard_map(
        per_device,
        mesh=mesh,
        in_specs=(
            P(None, "fsdp", "grp"),
            P(None, "fsdp", "grp"),
            P(None, "fsdp", "grp"),
            P(None, "fsdp", "grp"),
            P(None, "fsdp", "grp"),
            P(),
            P(),
            P(),
        ),
        out_specs=(
            P("fsdp", None, None, "grp"),
            P("fsdp", None, None, "grp"),
            P(None, "fsdp", "grp"),
        ),
        check_vma=False,
    )
```

```python
import functools

import jax
import jax.numpy as jnp
from jax import lax
from jax.experimental import pallas as pl
from jax.experimental.pallas import tpu as pltpu
from jax.sharding import PartitionSpec as P

MOST = 2
TILE = 128
SLAB = 8
HIGHEST = lax.Precision.HIGHEST
BF16 = jnp.bfloat16
F32 = jnp.float32


def lane_copy(tile, lane):
    return jnp.broadcast_to(tile[:, lane : lane + 1], (SLAB, TILE))


def row_copy(tile, row):
    return jnp.broadcast_to(tile[row : row + 1, :], (SLAB, TILE))


def tile_inverse(rows):
    lane = lax.broadcasted_iota(jnp.int32, (SLAB, TILE), 1)
    sub = lax.broadcasted_iota(jnp.int32, (SLAB, TILE), 0)
    count = len(rows)
    diagonal = [lane == sub + SLAB * s for s in range(count)]
    marked = [jnp.where(diagonal[s], rows[s], 0.0) for s in range(count)]
    while len(marked) > 1:
        marked = [marked[i] + marked[i + 1] for i in range(0, len(marked), 2)]
    across = lax.rsqrt(jnp.broadcast_to(jnp.sum(marked[0], axis=0, keepdims=True), (SLAB, TILE)))
    down = [
        jnp.broadcast_to(
            jnp.sum(jnp.where(diagonal[s], across, 0.0), axis=1, keepdims=True), (SLAB, TILE)
        )
        for s in range(count)
    ]
    rows = [rows[s] * across * down[s] for s in range(count)]
    for s in range(count):
        start = SLAB * s
        inside = (lane >= start) & (lane < start + SLAB)
        columns = [lane_copy(rows[s], start + c) for c in range(SLAB)]
        forward = jnp.where(inside, (lane - start == sub).astype(F32), rows[s])
        full = forward
        for k in range(0, SLAB, 2):
            first = columns[k]
            second = columns[k + 1]
            a = row_copy(first, k)
            b = row_copy(second, k)
            c = row_copy(second, k + 1)
            det = a * c - b * b
            pair = (sub == k) | (sub == k + 1)
            first = jnp.where(sub == k, -1.0, jnp.where(sub == k + 1, 0.0, first))
            second = jnp.where(sub == k + 1, -1.0, jnp.where(sub == k, 0.0, second))

            def parts(value):
                upper = row_copy(value, k)
                lower = row_copy(value, k + 1)
                reduced = a * lower - b * upper
                change = first * (c * upper - b * lower) + second * reduced
                return jnp.where(pair, 0.0, value), change, upper, reduced

            later = [parts(columns[q]) for q in range(k + 2, SLAB)]
            below = parts(forward)
            both = parts(full)
            inverse_det = 1.0 / det
            inverse_root = lax.rsqrt(a)
            for q, (kept, change, _, _) in enumerate(later):
                columns[k + 2 + q] = kept - change * inverse_det
            full = both[0] - both[1] * inverse_det
            forward = jnp.where(sub > k + 1, below[0] - below[1] * inverse_det, forward)
            forward = jnp.where(sub == k, below[2] * inverse_root, forward)
            forward = jnp.where(
                sub == k + 1, below[3] * (inverse_root * lax.rsqrt(det)), forward
            )
        rows[s] = forward
        if s + 1 < count:
            spread = [row_copy(full, j) for j in range(SLAB)]
        for i in range(s + 1, count):
            total = jnp.where(inside, 0.0, rows[i])
            for j in range(SLAB):
                total = total - lane_copy(rows[i], start + j) * spread[j]
            rows[i] = total
    return [jnp.where(lane <= sub + SLAB * s, rows[s] * across, 0.0) for s in range(count)]


def dot32(a, b, dims=((1,), (0,))):
    return lax.dot_general(a, b, (dims, ((), ())), precision=HIGHEST, preferred_element_type=F32)


def dot(a, b, dims=((1,), (0,))):
    return lax.dot_general(a, b, (dims, ((), ())), preferred_element_type=F32)


def read_slabs(tile_ref):
    return [tile_ref[SLAB * i : SLAB * (i + 1), :] for i in range(TILE // SLAB)]


def write_slabs(tile_ref, slabs):
    for i, slab in enumerate(slabs):
        tile_ref[SLAB * i : SLAB * (i + 1), :] = slab


def split3(value):
    high = value.astype(BF16)
    rest = value - high.astype(F32)
    middle = rest.astype(BF16)
    return high, middle, (rest - middle.astype(F32)).astype(BF16)


def left6(value):
    high, middle, small = split3(value)
    return jnp.concatenate([high, high, middle, middle, high, small], axis=1)


def right6(value, axis=0):
    high, middle, small = split3(value)
    return jnp.concatenate([high, middle, high, middle, small, high], axis=axis)


def invert(mat, tile, row, low):
    order = mat.shape[0]
    chunk = 256
    tile[...] = mat[:TILE, :TILE]
    write_slabs(tile, tile_inverse(read_slabs(tile)))
    lanes = lax.broadcasted_iota(jnp.int32, (TILE, order), 1)

    row_ids = lax.broadcasted_iota(jnp.int32, (order, TILE), 0)

    def step(k, carry):
        start = pl.multiple_of(k * TILE, TILE)
        after = pl.multiple_of(start + TILE, TILE)
        own = pl.ds(start, TILE)
        following = pl.ds(after, TILE)
        inverse = tile[...]
        near_upper = dot32(inverse, mat[own, following])
        near_side = dot32(mat[following, own], inverse, ((1,), (1,)))
        tile[...] = mat[following, following] - dot32(near_side, near_upper)
        row[...] = dot(left6(inverse), right6(mat[own, :]))
        row[:, own] = inverse
        column = mat[:, own]
        low[...] = jnp.where(row_ids >= after, dot(left6(column), right6(inverse, 1), ((1,), (1,))), 0.0)
        mat[:, own] = jnp.where(row_ids >= after, 0.0, column)
        mat[own, :] = jnp.where(lanes < after, row[...], 0.0)
        slabs = read_slabs(tile)
        lower = left6(low[...])
        upper = right6(row[...])
        for c in range(0, order, chunk):
            mat[:, c : c + chunk] -= dot(lower, upper[:, c : c + chunk])
        write_slabs(tile, tile_inverse(slabs))
        return carry

    lax.fori_loop(0, order // TILE - 1, step, 0)
    last = order - TILE
    inverse = tile[...]
    mat[last:, :] = dot32(inverse, mat[last:, :])
    mat[last:, last:] = inverse


def split32(value):
    high = value.astype(BF16)
    return high, (value - high.astype(F32)).astype(BF16)


def collect(group, pieces, targets):
    own, following, previous, far_top, far_bottom = pieces
    half, width = far_top.shape
    halves = [[piece.at[pl.ds(half * t, half), :] for t in range(2)] for piece in (own, following, previous)]
    for shift, pair in zip((0, 1, 3, 2), halves + [[far_top, far_bottom]]):
        columns = pl.ds(pl.multiple_of(lax.rem(group + shift, 4) * width, TILE), width)
        for source, target in zip(pair, targets):
            target[:, columns] = source[...]


def power_gram(group, pieces, factor, basis, power, mat):
    order, width = pieces[3].shape
    collect(group, pieces, (factor, basis))
    for c in range(0, order, width):
        power[:, c : c + width] = dot(factor[...], basis[:, c : c + width]).astype(BF16)
    for c in range(0, order, width):
        mat[:, c : c + width] = dot(power[...], power[:, c : c + width], ((0,), (0,)))


def fresh_of(power, inverse_rows):
    across = ((1,), (1,))
    high, low_part = split32(inverse_rows)
    total = dot(power[...], high, across) + dot(power[...], low_part, across)
    return total.astype(BF16)


def left_kernel(first, *refs):
    pieces, (fresh, mixer, factor, basis, power, mat), work = refs[:5], refs[5:11], refs[11:]
    power_gram(first[0], pieces, factor, basis, power, mat)
    invert(mat, *work)
    fresh[...] = fresh_of(power, mat[...])
    mixer[...] = dot(fresh[...], basis[...], ((0,), (0,))).astype(BF16)


def right_kernel(first, *refs):
    pieces, moment_pieces, mixer = refs[:5], refs[5:10], refs[10]
    (fresh, out, factor, basis, power, mat, moment), work = refs[11:18], refs[18:]
    group = first[0]
    half = moment.shape[0] // 2
    width = fresh.shape[1]
    power_gram(group, pieces, factor, basis, power, mat)
    collect(group, moment_pieces, [moment.at[pl.ds(half * t, half), :] for t in range(2)])
    carried = dot(moment[...], basis[...], ((1,), (1,))).astype(BF16)
    moment[...] = carried
    invert(mat, *work)
    fresh[...] = fresh_of(power, mat[pl.ds(pl.multiple_of(group * width, TILE), width), :])
    turned = dot(moment[...], fresh[...]).astype(BF16)
    out[...] = dot(mixer[...], turned).astype(BF16)


VMEM = pl.BlockSpec(memory_space=pltpu.VMEM)
SMEM = pl.BlockSpec(memory_space=pltpu.SMEM)


def basis_call(kernel, group_index, inputs, order, out_shapes, extra, name):
    square = pltpu.VMEM((order, order), BF16)
    return pl.pallas_call(
        kernel,
        out_shape=tuple(jax.ShapeDtypeStruct(shape, BF16) for shape in out_shapes),
        in_specs=[SMEM] + [VMEM] * len(inputs),
        out_specs=(VMEM,) * len(out_shapes),
        scratch_shapes=[square, square, square, pltpu.VMEM((order, order), F32)]
        + extra
        + [
            pltpu.VMEM((TILE, TILE), F32),
            pltpu.VMEM((TILE, order), F32),
            pltpu.VMEM((order, TILE), F32),
        ],
        compiler_params=pltpu.CompilerParams(vmem_limit_bytes=40 * 2**20),
        cost_estimate=pl.CostEstimate(
            flops=5 * 10**7 * order, bytes_accessed=10 * order**2, transcendentals=0
        ),
        name=name,
    )(group_index, *inputs)


def left_call(group_index, pieces):
    order = pieces[3].shape[0]
    shapes = [(order, order)] * 2
    return basis_call(left_kernel, group_index, pieces, order, shapes, [], "left_basis")


def right_call(group_index, pieces, moment_pieces, mixer):
    order, width = pieces[3].shape
    rows = mixer.shape[0]
    return basis_call(
        right_kernel,
        group_index,
        (*pieces, *moment_pieces, mixer),
        order,
        [(order, width), (rows, width)],
        [pltpu.VMEM((rows, order), BF16)],
        "right_basis",
    )


def pack_kernel(places, blocks, row_extent, col_extent, factor_r, factor_l, basis_r, basis_l, moment, out):
    rows_r, cols_r = factor_r.shape[1:]
    rows_l, cols_l = factor_l.shape[1:]

    def ids(rows, cols):
        return (
            lax.broadcasted_iota(jnp.int32, (rows, cols), 0) + places[0] * rows,
            lax.broadcasted_iota(jnp.int32, (rows, cols), 1) + places[1] * cols,
        )

    row_r, col_r = ids(rows_r, cols_r)
    row_l, col_l = ids(rows_l, cols_l)
    unit_r = (row_r == col_r).astype(F32)
    unit_l = (row_l == col_l).astype(F32)
    most_r = jnp.maximum(row_r, col_r)
    most_l = jnp.maximum(row_l, col_l)

    def step(r, carry):
        b = jnp.clip(blocks[r], 0, factor_r.shape[0] - 1)
        masked = jnp.where(most_r < col_extent[b], factor_r[b].astype(F32), unit_r)
        out[r, :rows_r, :] = masked.astype(BF16)
        out[r, rows_r : 2 * rows_r, :] = basis_r[b].astype(BF16)
        masked = jnp.where(most_l < row_extent[b], factor_l[b].astype(F32), unit_l)
        left = jnp.concatenate([masked, basis_l[b]], axis=1)
        both = jnp.concatenate([left, moment[b].astype(F32)], axis=0)
        out[r, 2 * rows_r :, :] = both.astype(BF16)
        return carry

    lax.fori_loop(0, out.shape[0], step, 0)


def packed(places, blocks, row_extent, col_extent, *arrays):
    rows_r, cols_r = arrays[0].shape[1:]
    rows_l = arrays[1].shape[1]
    return pl.pallas_call(
        pack_kernel,
        out_shape=jax.ShapeDtypeStruct(
            (blocks.shape[0], 2 * rows_r + 2 * rows_l, cols_r), BF16
        ),
        in_specs=[SMEM] * 4 + [VMEM] * 5,
        out_specs=VMEM,
        compiler_params=pltpu.CompilerParams(vmem_limit_bytes=24 * 2**20),
        cost_estimate=pl.CostEstimate(flops=10**9, bytes_accessed=4 * 2**20, transcendentals=0),
        name="packed",
    )(places, blocks, row_extent, col_extent, *arrays)


def shifted(piece, shift):
    count = lax.axis_size("grp")
    return lax.ppermute(piece, "grp", [(i, (i + shift) % count) for i in range(count)])


def near(piece):
    return shifted(piece, 1), shifted(piece, -1)


def gathered(piece, previous, following):
    half = piece.shape[0] // 2
    return piece, following, previous, shifted(previous[:half], 1), shifted(following[half:], -1)


def gathered_at_once(piece):
    half = piece.shape[0] // 2
    return (
        piece,
        shifted(piece, -1),
        shifted(piece, 1),
        shifted(piece[:half], 2),
        shifted(piece[half:], -2),
    )


def eye_piece(row_count, col_count, col_start):
    row_ids = lax.broadcasted_iota(jnp.int32, (row_count, col_count), 0)
    col_ids = lax.broadcasted_iota(jnp.int32, (row_count, col_count), 1) + col_start
    return (row_ids == col_ids).astype(F32)


def placement(owner, owner_count):
    block_ids = jnp.arange(owner.shape[0], dtype=jnp.int32)
    rows = jnp.arange(owner_count, dtype=jnp.int32)

    def total(hits, values):
        return jnp.sum(jnp.where(hits, values, 0), axis=1)

    earlier = (owner[:, None] == owner[None, :]) & (block_ids[None, :] < block_ids[:, None])
    repeated = jnp.any(earlier, axis=1)
    owned = rows[:, None] == owner[None, :]
    first_hits = owned & ~repeated[None, :]
    second_hits = owned & repeated[None, :]
    has_first = jnp.any(first_hits, axis=1)
    has_second = jnp.any(second_hits, axis=1)
    before = rows[None, :] < rows[:, None]
    empty_rank = total(before & ~has_first[None, :], 1)
    double_rank = total(before & has_second[None, :], 1)
    matched = ~has_first[:, None] & has_second[None, :] & (empty_rank[:, None] == double_rank[None, :])
    second_of = total(second_hits, block_ids[None, :])
    row_block = total(first_hits, block_ids[None, :]) + total(matched, second_of[None, :])
    second_row = jnp.sum(jnp.where(matched, rows[:, None], 0), axis=0)
    row_of = total(block_ids[:, None] == row_block[None, :], rows[None, :])
    return (row_block, row_of, second_row, has_first, has_second)


def pick(values, indices):
    return jnp.take(values, indices, axis=0, mode="clip")


def swap(pieces):
    return lax.all_to_all(pieces, "fsdp", split_axis=0, concat_axis=0, tiled=True)


def per_device(
    right_factor, left_factor, right_basis, left_basis, moment, owner, row_extent, col_extent
):
    owner_count = lax.axis_size("fsdp")
    fsdp_index = lax.axis_index("fsdp")
    group_index = lax.axis_index("grp")
    right_rows, right_cols = right_factor.shape[1:]
    left_rows, left_cols = left_factor.shape[1:]
    order_r = right_rows * owner_count
    order_l = left_rows * owner_count
    row_block, row_of, second_row, has_first, has_second = placement(owner, owner_count)
    group = group_index.astype(jnp.int32)[None]
    places = jnp.stack([fsdp_index, group_index]).astype(jnp.int32)
    pack = packed(
        places,
        row_block,
        row_extent,
        col_extent,
        right_factor,
        left_factor,
        right_basis,
        left_basis,
        moment,
    )
    pack = swap(pack)
    bounds = (0, right_rows, 2 * right_rows, 2 * right_rows + left_rows, 2 * (right_rows + left_rows))
    factor_r, basis_r, left_pair, moment_in = (
        pack[:, start:stop].reshape(-1, right_cols) for start, stop in zip(bounds, bounds[1:])
    )
    left_piece = jnp.concatenate([left_pair[:, :left_cols], left_pair[:, left_cols:]], axis=0)
    right_piece = jnp.concatenate([factor_r, basis_r], axis=0)

    left_pieces = gathered(left_piece, *near(left_piece))
    left_pieces, right_piece = lax.optimization_barrier((left_pieces, right_piece))
    right_near = near(right_piece)
    fresh_l, mixer = left_call(group, left_pieces)
    fresh_l, right_near = lax.optimization_barrier((fresh_l, right_near))
    left_new = lax.dynamic_slice_in_dim(fresh_l, group_index * left_cols, left_cols, 1)
    rows_l = swap(left_new.reshape(owner_count, left_rows, left_cols))
    right_near, moment_in = lax.optimization_barrier((right_near, moment_in))
    right_pieces = gathered(right_piece, *right_near)
    moment_pieces = gathered_at_once(moment_in)
    fresh_r, moment_out = right_call(group, right_pieces, moment_pieces, mixer)
    fresh_r, rows_l = lax.optimization_barrier((fresh_r, rows_l))

    by_row = fresh_r.reshape(owner_count, MOST, left_rows, right_cols)
    back = jnp.concatenate(
        [
            by_row[:, 0],
            by_row[:, 1],
            moment_out.reshape(owner_count, left_rows, right_cols),
            pick(rows_l, second_row),
        ],
        axis=2,
    )
    back = swap(back)
    wide = MOST * right_cols
    second_r = swap(pick(back[:, :, :wide], second_row))
    second_r = jnp.stack([second_r[:, :, :right_cols], second_r[:, :, right_cols:]], axis=1)
    second_r = second_r.reshape(order_r, right_cols)
    second_l = back[:, :, wide + right_cols :].reshape(order_l, left_cols)
    new_moment = pick(back[:, :, wide : wide + right_cols], row_of)

    def slots(own, second):
        order, width = own.shape
        unit = eye_piece(order, width, group_index * width)
        filled = (
            lax.dynamic_index_in_dim(has, fsdp_index, keepdims=False)
            for has in (has_first, has_second)
        )
        pair = [jnp.where(has, new.astype(F32), unit) for has, new in zip(filled, (own, second))]
        return jnp.stack(pair)[None]

    return (slots(fresh_r, second_r), slots(left_new, second_l), new_moment)


def solution(mesh):
    return jax.shard_map(
        per_device,
        mesh=mesh,
        in_specs=(
            P(None, "fsdp", "grp"),
            P(None, "fsdp", "grp"),
            P(None, "fsdp", "grp"),
            P(None, "fsdp", "grp"),
            P(None, "fsdp", "grp"),
            P(),
            P(),
            P(),
        ),
        out_specs=(
            P("fsdp", None, None, "grp"),
            P("fsdp", None, None, "grp"),
            P(None, "fsdp", "grp"),
        ),
        check_vma=False,
    )
```

```python
import functools

import jax
import jax.numpy as jnp
from jax import lax
from jax.experimental import pallas as pl
from jax.experimental.pallas import tpu as pltpu
from jax.sharding import PartitionSpec as P

MOST = 2
TILE = 128
SLAB = 8
HIGHEST = lax.Precision.HIGHEST
BF16 = jnp.bfloat16
F32 = jnp.float32


def lane_copy(tile, lane):
    return jnp.broadcast_to(tile[:, lane : lane + 1], (SLAB, TILE))


def row_copy(tile, row):
    return jnp.broadcast_to(tile[row : row + 1, :], (SLAB, TILE))


def tile_inverse(rows):
    lane = lax.broadcasted_iota(jnp.int32, (SLAB, TILE), 1)
    sub = lax.broadcasted_iota(jnp.int32, (SLAB, TILE), 0)
    count = len(rows)
    diagonal = [lane == sub + SLAB * s for s in range(count)]
    marked = [jnp.where(diagonal[s], rows[s], 0.0) for s in range(count)]
    while len(marked) > 1:
        marked = [marked[i] + marked[i + 1] for i in range(0, len(marked), 2)]
    across = lax.rsqrt(jnp.broadcast_to(jnp.sum(marked[0], axis=0, keepdims=True), (SLAB, TILE)))
    down = [
        jnp.broadcast_to(
            jnp.sum(jnp.where(diagonal[s], across, 0.0), axis=1, keepdims=True), (SLAB, TILE)
        )
        for s in range(count)
    ]
    rows = [rows[s] * across * down[s] for s in range(count)]
    for s in range(count):
        start = SLAB * s
        inside = (lane >= start) & (lane < start + SLAB)
        columns = [lane_copy(rows[s], start + c) for c in range(SLAB)]
        forward = jnp.where(inside, (lane - start == sub).astype(F32), rows[s])
        full = forward
        for k in range(0, SLAB, 2):
            first = columns[k]
            second = columns[k + 1]
            a = row_copy(first, k)
            b = row_copy(second, k)
            c = row_copy(second, k + 1)
            det = a * c - b * b
            pair = (sub == k) | (sub == k + 1)
            first = jnp.where(sub == k, -1.0, jnp.where(sub == k + 1, 0.0, first))
            second = jnp.where(sub == k + 1, -1.0, jnp.where(sub == k, 0.0, second))

            def parts(value):
                upper = row_copy(value, k)
                lower = row_copy(value, k + 1)
                reduced = a * lower - b * upper
                change = first * (c * upper - b * lower) + second * reduced
                return jnp.where(pair, 0.0, value), change, upper, reduced

            later = [parts(columns[q]) for q in range(k + 2, SLAB)]
            below = parts(forward)
            both = parts(full)
            inverse_det = 1.0 / det
            inverse_root = lax.rsqrt(a)
            for q, (kept, change, _, _) in enumerate(later):
                columns[k + 2 + q] = kept - change * inverse_det
            full = both[0] - both[1] * inverse_det
            forward = jnp.where(sub > k + 1, below[0] - below[1] * inverse_det, forward)
            forward = jnp.where(sub == k, below[2] * inverse_root, forward)
            forward = jnp.where(
                sub == k + 1, below[3] * (inverse_root * lax.rsqrt(det)), forward
            )
        rows[s] = forward
        if s + 1 < count:
            spread = [row_copy(full, j) for j in range(SLAB)]
        for i in range(s + 1, count):
            total = jnp.where(inside, 0.0, rows[i])
            for j in range(SLAB):
                total = total - lane_copy(rows[i], start + j) * spread[j]
            rows[i] = total
    return [jnp.where(lane <= sub + SLAB * s, rows[s] * across, 0.0) for s in range(count)]


def dot32(a, b, dims=((1,), (0,))):
    return lax.dot_general(a, b, (dims, ((), ())), precision=HIGHEST, preferred_element_type=F32)


def dot(a, b, dims=((1,), (0,))):
    return lax.dot_general(a, b, (dims, ((), ())), preferred_element_type=F32)


def read_slabs(tile_ref):
    return [tile_ref[SLAB * i : SLAB * (i + 1), :] for i in range(TILE // SLAB)]


def write_slabs(tile_ref, slabs):
    for i, slab in enumerate(slabs):
        tile_ref[SLAB * i : SLAB * (i + 1), :] = slab


def split3(value):
    high = value.astype(BF16)
    rest = value - high.astype(F32)
    middle = rest.astype(BF16)
    return high, middle, (rest - middle.astype(F32)).astype(BF16)


def left6(value):
    high, middle, small = split3(value)
    return jnp.concatenate([high, high, middle, middle, high, small], axis=1)


def right6(value, axis=0):
    high, middle, small = split3(value)
    return jnp.concatenate([high, middle, high, middle, small, high], axis=axis)


def invert(mat, tile, row, low):
    order = mat.shape[0]
    chunk = 256
    tile[...] = mat[:TILE, :TILE]
    write_slabs(tile, tile_inverse(read_slabs(tile)))
    lanes = lax.broadcasted_iota(jnp.int32, (TILE, order), 1)

    row_ids = lax.broadcasted_iota(jnp.int32, (order, TILE), 0)

    def step(k, carry):
        start = pl.multiple_of(k * TILE, TILE)
        after = pl.multiple_of(start + TILE, TILE)
        own = pl.ds(start, TILE)
        following = pl.ds(after, TILE)
        inverse = tile[...]
        near_upper = dot32(inverse, mat[own, following])
        near_side = dot32(mat[following, own], inverse, ((1,), (1,)))
        tile[...] = mat[following, following] - dot32(near_side, near_upper)
        row[...] = dot(left6(inverse), right6(mat[own, :]))
        row[:, own] = inverse
        column = mat[:, own]
        low[...] = jnp.where(row_ids >= after, dot(left6(column), right6(inverse, 1), ((1,), (1,))), 0.0)
        mat[:, own] = jnp.where(row_ids >= after, 0.0, column)
        mat[own, :] = jnp.where(lanes < after, row[...], 0.0)
        slabs = read_slabs(tile)
        lower = left6(low[...])
        upper = right6(row[...])
        for c in range(0, order, chunk):
            mat[:, c : c + chunk] -= dot(lower, upper[:, c : c + chunk])
        write_slabs(tile, tile_inverse(slabs))
        return carry

    lax.fori_loop(0, order // TILE - 1, step, 0)
    last = order - TILE
    inverse = tile[...]
    mat[last:, :] = dot32(inverse, mat[last:, :])
    mat[last:, last:] = inverse


def split32(value):
    high = value.astype(BF16)
    return high, (value - high.astype(F32)).astype(BF16)


def collect(group, pieces, tops, bottoms):
    own, following, previous, far_top, far_bottom = pieces
    half, width = far_top.shape
    for shift, piece in ((0, own), (1, following), (3, previous), (2, None)):
        columns = pl.ds(pl.multiple_of(lax.rem(group + shift, 4) * width, TILE), width)
        for part, targets in enumerate((tops, bottoms)):
            source = (far_top, far_bottom)[part] if piece is None else piece
            start = 0 if piece is None else part * half
            for target in targets:
                rows = target.shape[0]
                target[:, columns] = source[start : start + rows, :]
                start += rows


def power_gram(width, factor, basis, power, mat):
    order = mat.shape[0]
    for c in range(0, order, width):
        power[:, c : c + width] = dot(factor[...], basis[:, c : c + width]).astype(BF16)
    for c in range(0, order, width):
        mat[:, c : c + width] = dot(power[...], power[:, c : c + width], ((0,), (0,)))


def fresh_of(power, inverse_rows):
    across = ((1,), (1,))
    high, low_part = split32(inverse_rows)
    total = dot(power[...], high, across) + dot(power[...], low_part, across)
    return total.astype(BF16)


def left_kernel(first, *refs):
    pieces, (fresh, mixer, factor, basis, power, mat), work = refs[:5], refs[5:11], refs[11:]
    collect(first[0], pieces, (factor,), (basis,))
    power_gram(pieces[3].shape[1], factor, basis, power, mat)
    invert(mat, *work)
    fresh[...] = fresh_of(power, mat[...])
    mixer[...] = dot(fresh[...], basis[...], ((0,), (0,))).astype(BF16)


def right_kernel(first, *refs):
    pieces, mixer = refs[:5], refs[5]
    (fresh, out, factor, basis, power, mat, moment), work = refs[6:13], refs[13:]
    group = first[0]
    half = moment.shape[0] // 2
    width = fresh.shape[1]
    upper, lower = (moment.at[pl.ds(half * t, half), :] for t in range(2))
    collect(group, pieces, (factor, upper), (basis, lower))
    power_gram(width, factor, basis, power, mat)
    carried = dot(moment[...], basis[...], ((1,), (1,))).astype(BF16)
    moment[...] = carried
    invert(mat, *work)
    fresh[...] = fresh_of(power, mat[pl.ds(pl.multiple_of(group * width, TILE), width), :])
    turned = dot(moment[...], fresh[...]).astype(BF16)
    out[...] = dot(mixer[...], turned).astype(BF16)


VMEM = pl.BlockSpec(memory_space=pltpu.VMEM)
SMEM = pl.BlockSpec(memory_space=pltpu.SMEM)


def basis_call(kernel, group_index, inputs, order, out_shapes, extra, vmem, name):
    square = pltpu.VMEM((order, order), BF16)
    return pl.pallas_call(
        kernel,
        out_shape=tuple(jax.ShapeDtypeStruct(shape, BF16) for shape in out_shapes),
        in_specs=[SMEM] + [VMEM] * len(inputs),
        out_specs=(VMEM,) * len(out_shapes),
        scratch_shapes=[square, square, square, pltpu.VMEM((order, order), F32)]
        + extra
        + [
            pltpu.VMEM((TILE, TILE), F32),
            pltpu.VMEM((TILE, order), F32),
            pltpu.VMEM((order, TILE), F32),
        ],
        compiler_params=pltpu.CompilerParams(vmem_limit_bytes=vmem * 2**20),
        cost_estimate=pl.CostEstimate(
            flops=5 * 10**7 * order, bytes_accessed=10 * order**2, transcendentals=0
        ),
        name=name,
    )(group_index, *inputs)


def left_call(group_index, pieces):
    order = pieces[3].shape[0]
    shapes = [(order, order)] * 2
    return basis_call(left_kernel, group_index, pieces, order, shapes, [], 40, "left_basis")


def right_call(group_index, pieces, mixer):
    rows = mixer.shape[0]
    order, width = pieces[3].shape
    order -= rows // 2
    return basis_call(
        right_kernel,
        group_index,
        (*pieces, mixer),
        order,
        [(order, width), (rows, width)],
        [pltpu.VMEM((rows, order), BF16)],
        56,
        "right_basis",
    )


def pack_kernel(places, blocks, row_extent, col_extent, factor_r, factor_l, basis_r, basis_l, moment, out):
    rows_r, cols_r = factor_r.shape[1:]
    rows_l, cols_l = factor_l.shape[1:]

    def ids(rows, cols):
        return (
            lax.broadcasted_iota(jnp.int32, (rows, cols), 0) + places[0] * rows,
            lax.broadcasted_iota(jnp.int32, (rows, cols), 1) + places[1] * cols,
        )

    row_r, col_r = ids(rows_r, cols_r)
    row_l, col_l = ids(rows_l, cols_l)
    unit_r = (row_r == col_r).astype(F32)
    unit_l = (row_l == col_l).astype(F32)
    most_r = jnp.maximum(row_r, col_r)
    most_l = jnp.maximum(row_l, col_l)

    def step(r, carry):
        b = jnp.clip(blocks[r], 0, factor_r.shape[0] - 1)
        masked = jnp.where(most_r < col_extent[b], factor_r[b].astype(F32), unit_r)
        out[r, :rows_r, :] = masked.astype(BF16)
        out[r, rows_r : 2 * rows_r, :] = basis_r[b].astype(BF16)
        masked = jnp.where(most_l < row_extent[b], factor_l[b].astype(F32), unit_l)
        left = jnp.concatenate([masked, basis_l[b]], axis=1)
        both = jnp.concatenate([left, moment[b].astype(F32)], axis=0)
        out[r, 2 * rows_r :, :] = both.astype(BF16)
        return carry

    lax.fori_loop(0, out.shape[0], step, 0)


def packed(places, blocks, row_extent, col_extent, *arrays):
    rows_r, cols_r = arrays[0].shape[1:]
    rows_l = arrays[1].shape[1]
    return pl.pallas_call(
        pack_kernel,
        out_shape=jax.ShapeDtypeStruct(
            (blocks.shape[0], 2 * rows_r + 2 * rows_l, cols_r), BF16
        ),
        in_specs=[SMEM] * 4 + [VMEM] * 5,
        out_specs=VMEM,
        compiler_params=pltpu.CompilerParams(vmem_limit_bytes=56 * 2**20),
        cost_estimate=pl.CostEstimate(flops=10**9, bytes_accessed=4 * 2**20, transcendentals=0),
        name="packed",
    )(places, blocks, row_extent, col_extent, *arrays)


def shifted(piece, shift):
    count = lax.axis_size("grp")
    return lax.ppermute(piece, "grp", [(i, (i + shift) % count) for i in range(count)])


def near(piece):
    return shifted(piece, 1), shifted(piece, -1)


def gathered(piece, previous, following):
    half = piece.shape[0] // 2
    return piece, following, previous, shifted(previous[:half], 1), shifted(following[half:], -1)


def eye_piece(row_count, col_count, col_start):
    row_ids = lax.broadcasted_iota(jnp.int32, (row_count, col_count), 0)
    col_ids = lax.broadcasted_iota(jnp.int32, (row_count, col_count), 1) + col_start
    return (row_ids == col_ids).astype(F32)


def placement(owner, owner_count):
    block_ids = jnp.arange(owner.shape[0], dtype=jnp.int32)
    rows = jnp.arange(owner_count, dtype=jnp.int32)

    def total(hits, values):
        return jnp.sum(jnp.where(hits, values, 0), axis=1)

    earlier = (owner[:, None] == owner[None, :]) & (block_ids[None, :] < block_ids[:, None])
    repeated = jnp.any(earlier, axis=1)
    owned = rows[:, None] == owner[None, :]
    first_hits = owned & ~repeated[None, :]
    second_hits = owned & repeated[None, :]
    has_first = jnp.any(first_hits, axis=1)
    has_second = jnp.any(second_hits, axis=1)
    before = rows[None, :] < rows[:, None]
    empty_rank = total(before & ~has_first[None, :], 1)
    double_rank = total(before & has_second[None, :], 1)
    matched = ~has_first[:, None] & has_second[None, :] & (empty_rank[:, None] == double_rank[None, :])
    second_of = total(second_hits, block_ids[None, :])
    row_block = total(first_hits, block_ids[None, :]) + total(matched, second_of[None, :])
    second_row = jnp.sum(jnp.where(matched, rows[:, None], 0), axis=0)
    row_of = total(block_ids[:, None] == row_block[None, :], rows[None, :])
    return (row_block, row_of, second_row, has_first, has_second)


def pick(values, indices):
    return jnp.take(values, indices, axis=0, mode="clip")


def swap(pieces):
    return lax.all_to_all(pieces, "fsdp", split_axis=0, concat_axis=0, tiled=True)


def per_device(
    right_factor, left_factor, right_basis, left_basis, moment, owner, row_extent, col_extent
):
    owner_count = lax.axis_size("fsdp")
    fsdp_index = lax.axis_index("fsdp")
    group_index = lax.axis_index("grp")
    right_rows, right_cols = right_factor.shape[1:]
    left_rows, left_cols = left_factor.shape[1:]
    order_r = right_rows * owner_count
    order_l = left_rows * owner_count
    row_block, row_of, second_row, has_first, has_second = placement(owner, owner_count)
    group = group_index.astype(jnp.int32)[None]
    places = jnp.stack([fsdp_index, group_index]).astype(jnp.int32)
    pack = packed(
        places,
        row_block,
        row_extent,
        col_extent,
        right_factor,
        left_factor,
        right_basis,
        left_basis,
        moment,
    )
    pack = swap(pack)
    bounds = (0, right_rows, 2 * right_rows, 2 * right_rows + left_rows, 2 * (right_rows + left_rows))
    factor_r, basis_r, left_pair, moment_in = (
        pack[:, start:stop].reshape(-1, right_cols) for start, stop in zip(bounds, bounds[1:])
    )
    left_piece = jnp.concatenate([left_pair[:, :left_cols], left_pair[:, left_cols:]], axis=0)
    half = order_l // 2
    right_piece = jnp.concatenate([factor_r, moment_in[:half], basis_r, moment_in[half:]], axis=0)

    left_pieces = gathered(left_piece, *near(left_piece))
    left_pieces, right_piece = lax.optimization_barrier((left_pieces, right_piece))
    right_near = near(right_piece)
    fresh_l, mixer = left_call(group, left_pieces)
    fresh_l, right_near = lax.optimization_barrier((fresh_l, right_near))
    left_new = lax.dynamic_slice_in_dim(fresh_l, group_index * left_cols, left_cols, 1)
    rows_l = swap(left_new.reshape(owner_count, left_rows, left_cols))
    right_pieces = gathered(right_piece, *right_near)
    fresh_r, moment_out = right_call(group, right_pieces, mixer)
    fresh_r, rows_l = lax.optimization_barrier((fresh_r, rows_l))

    by_row = fresh_r.reshape(owner_count, MOST, left_rows, right_cols)
    back = jnp.concatenate(
        [
            by_row[:, 0],
            by_row[:, 1],
            moment_out.reshape(owner_count, left_rows, right_cols),
            pick(rows_l, second_row),
        ],
        axis=2,
    )
    back = swap(back)
    wide = MOST * right_cols
    second_r = swap(pick(back[:, :, :wide], second_row))
    second_r = jnp.stack([second_r[:, :, :right_cols], second_r[:, :, right_cols:]], axis=1)
    second_r = second_r.reshape(order_r, right_cols)
    second_l = back[:, :, wide + right_cols :].reshape(order_l, left_cols)
    new_moment = pick(back[:, :, wide : wide + right_cols], row_of)

    def slots(own, second):
        order, width = own.shape
        unit = eye_piece(order, width, group_index * width)
        filled = jnp.stack(
            [
                lax.dynamic_index_in_dim(has, fsdp_index, keepdims=False)
                for has in (has_first, has_second)
            ]
        )
        pair = jnp.stack([own, second]).astype(F32)
        return jnp.where(filled[:, None, None], pair, unit)[None]

    return (slots(fresh_r, second_r), slots(left_new, second_l), new_moment)


def solution(mesh):
    return jax.shard_map(
        per_device,
        mesh=mesh,
        in_specs=(
            P(None, "fsdp", "grp"),
            P(None, "fsdp", "grp"),
            P(None, "fsdp", "grp"),
            P(None, "fsdp", "grp"),
            P(None, "fsdp", "grp"),
            P(),
            P(),
            P(),
        ),
        out_specs=(
            P("fsdp", None, None, "grp"),
            P("fsdp", None, None, "grp"),
            P(None, "fsdp", "grp"),
        ),
        check_vma=False,
    )
```

```python
import functools

import jax
import jax.numpy as jnp
from jax import lax
from jax.experimental import pallas as pl
from jax.experimental.pallas import tpu as pltpu
from jax.sharding import PartitionSpec as P

MOST = 2
TILE = 128
SLAB = 8
HIGHEST = lax.Precision.HIGHEST
BF16 = jnp.bfloat16
F32 = jnp.float32


def lane_copy(tile, lane):
    return jnp.broadcast_to(tile[:, lane : lane + 1], (SLAB, TILE))


def row_copy(tile, row):
    return jnp.broadcast_to(tile[row : row + 1, :], (SLAB, TILE))


def tile_inverse(rows):
    lane = lax.broadcasted_iota(jnp.int32, (SLAB, TILE), 1)
    sub = lax.broadcasted_iota(jnp.int32, (SLAB, TILE), 0)
    count = len(rows)
    diagonal = [lane == sub + SLAB * s for s in range(count)]
    marked = [jnp.where(diagonal[s], rows[s], 0.0) for s in range(count)]
    while len(marked) > 1:
        marked = [marked[i] + marked[i + 1] for i in range(0, len(marked), 2)]
    across = lax.rsqrt(jnp.broadcast_to(jnp.sum(marked[0], axis=0, keepdims=True), (SLAB, TILE)))
    down = [
        jnp.broadcast_to(
            jnp.sum(jnp.where(diagonal[s], across, 0.0), axis=1, keepdims=True), (SLAB, TILE)
        )
        for s in range(count)
    ]
    rows = [rows[s] * across * down[s] for s in range(count)]
    for s in range(count):
        start = SLAB * s
        inside = (lane >= start) & (lane < start + SLAB)
        columns = [lane_copy(rows[s], start + c) for c in range(SLAB)]
        forward = jnp.where(inside, (lane - start == sub).astype(F32), rows[s])
        full = forward
        for k in range(0, SLAB, 2):
            first = columns[k]
            second = columns[k + 1]
            a = row_copy(first, k)
            b = row_copy(second, k)
            c = row_copy(second, k + 1)
            det = a * c - b * b
            pair = (sub == k) | (sub == k + 1)
            first = jnp.where(sub == k, -1.0, jnp.where(sub == k + 1, 0.0, first))
            second = jnp.where(sub == k + 1, -1.0, jnp.where(sub == k, 0.0, second))

            def parts(value):
                upper = row_copy(value, k)
                lower = row_copy(value, k + 1)
                reduced = a * lower - b * upper
                change = first * (c * upper - b * lower) + second * reduced
                return jnp.where(pair, 0.0, value), change, upper, reduced

            later = [parts(columns[q]) for q in range(k + 2, SLAB)]
            below = parts(forward)
            both = parts(full)
            inverse_det = 1.0 / det
            inverse_root = lax.rsqrt(a)
            for q, (kept, change, _, _) in enumerate(later):
                columns[k + 2 + q] = kept - change * inverse_det
            full = both[0] - both[1] * inverse_det
            forward = jnp.where(sub > k + 1, below[0] - below[1] * inverse_det, forward)
            forward = jnp.where(sub == k, below[2] * inverse_root, forward)
            forward = jnp.where(
                sub == k + 1, below[3] * (inverse_root * lax.rsqrt(det)), forward
            )
        rows[s] = forward
        if s + 1 < count:
            spread = [row_copy(full, j) for j in range(SLAB)]
        for i in range(s + 1, count):
            total = jnp.where(inside, 0.0, rows[i])
            for j in range(SLAB):
                total = total - lane_copy(rows[i], start + j) * spread[j]
            rows[i] = total
    return [jnp.where(lane <= sub + SLAB * s, rows[s] * across, 0.0) for s in range(count)]


def dot32(a, b, dims=((1,), (0,))):
    return lax.dot_general(a, b, (dims, ((), ())), precision=HIGHEST, preferred_element_type=F32)


def dot(a, b, dims=((1,), (0,))):
    return lax.dot_general(a, b, (dims, ((), ())), preferred_element_type=F32)


def read_slabs(tile_ref):
    return [tile_ref[SLAB * i : SLAB * (i + 1), :] for i in range(TILE // SLAB)]


def write_slabs(tile_ref, slabs):
    for i, slab in enumerate(slabs):
        tile_ref[SLAB * i : SLAB * (i + 1), :] = slab


def split3(value):
    high = value.astype(BF16)
    rest = value - high.astype(F32)
    middle = rest.astype(BF16)
    return high, middle, (rest - middle.astype(F32)).astype(BF16)


def left6(value):
    high, middle, small = split3(value)
    return jnp.concatenate([high, high, middle, middle, high, small], axis=1)


def right6(value, axis=0):
    high, middle, small = split3(value)
    return jnp.concatenate([high, middle, high, middle, small, high], axis=axis)


def invert(mat, tile, row, low):
    order = mat.shape[0]
    chunk = 256
    tile[...] = mat[:TILE, :TILE]
    write_slabs(tile, tile_inverse(read_slabs(tile)))
    lanes = lax.broadcasted_iota(jnp.int32, (TILE, order), 1)

    row_ids = lax.broadcasted_iota(jnp.int32, (order, TILE), 0)

    def step(k, carry):
        start = pl.multiple_of(k * TILE, TILE)
        after = pl.multiple_of(start + TILE, TILE)
        own = pl.ds(start, TILE)
        following = pl.ds(after, TILE)
        inverse = tile[...]
        near_upper = dot32(inverse, mat[own, following])
        near_side = dot32(mat[following, own], inverse, ((1,), (1,)))
        tile[...] = mat[following, following] - dot32(near_side, near_upper)
        row[...] = dot(left6(inverse), right6(mat[own, :]))
        row[:, own] = inverse
        column = mat[:, own]
        low[...] = jnp.where(row_ids >= after, dot(left6(column), right6(inverse, 1), ((1,), (1,))), 0.0)
        mat[:, own] = jnp.where(row_ids >= after, 0.0, column)
        mat[own, :] = jnp.where(lanes < after, row[...], 0.0)
        slabs = read_slabs(tile)
        lower = left6(low[...])
        upper = right6(row[...])
        for c in range(0, order, chunk):
            mat[:, c : c + chunk] -= dot(lower, upper[:, c : c + chunk])
        write_slabs(tile, tile_inverse(slabs))
        return carry

    lax.fori_loop(0, order // TILE - 1, step, 0)
    last = order - TILE
    inverse = tile[...]
    mat[last:, :] = dot32(inverse, mat[last:, :])
    mat[last:, last:] = inverse


def split32(value):
    high = value.astype(BF16)
    return high, (value - high.astype(F32)).astype(BF16)


def collect(group, pieces, tops, bottoms):
    own, following, previous, far_top, far_bottom = pieces
    half, width = far_top.shape
    for shift, piece in ((0, own), (1, following), (3, previous), (2, None)):
        columns = pl.ds(pl.multiple_of(lax.rem(group + shift, 4) * width, TILE), width)
        for part, targets in enumerate((tops, bottoms)):
            source = (far_top, far_bottom)[part] if piece is None else piece
            start = 0 if piece is None else part * half
            for target in targets:
                rows = target.shape[0]
                target[:, columns] = source[start : start + rows, :]
                start += rows


def power_gram(width, factor, basis, power, mat):
    order = mat.shape[0]
    for c in range(0, order, width):
        power[:, c : c + width] = dot(factor[...], basis[:, c : c + width]).astype(BF16)
    for c in range(0, order, width):
        mat[:, c : c + width] = dot(power[...], power[:, c : c + width], ((0,), (0,)))


def fresh_of(power, inverse_rows):
    across = ((1,), (1,))
    high, low_part = split32(inverse_rows)
    total = dot(power[...], high, across) + dot(power[...], low_part, across)
    return total.astype(BF16)


def left_kernel(first, *refs):
    pieces, (fresh, mixer, factor, basis, power, mat), work = refs[:5], refs[5:11], refs[11:]
    collect(first[0], pieces, (factor,), (basis,))
    power_gram(pieces[3].shape[1], factor, basis, power, mat)
    invert(mat, *work)
    fresh[...] = fresh_of(power, mat[...])
    mixer[...] = dot(fresh[...], basis[...], ((0,), (0,))).astype(BF16)


def right_kernel(first, *refs):
    pieces, mixer = refs[:5], refs[5]
    (fresh, out, factor, basis, power, mat, moment), work = refs[6:13], refs[13:]
    group = first[0]
    half = moment.shape[0] // 2
    width = fresh.shape[1]
    upper, lower = (moment.at[pl.ds(half * t, half), :] for t in range(2))
    collect(group, pieces, (factor, upper), (basis, lower))
    power_gram(width, factor, basis, power, mat)
    carried = dot(moment[...], basis[...], ((1,), (1,))).astype(BF16)
    moment[...] = carried
    invert(mat, *work)
    fresh[...] = fresh_of(power, mat[pl.ds(pl.multiple_of(group * width, TILE), width), :])
    turned = dot(moment[...], fresh[...]).astype(BF16)
    out[...] = dot(mixer[...], turned).astype(BF16)


VMEM = pl.BlockSpec(memory_space=pltpu.VMEM)
SMEM = pl.BlockSpec(memory_space=pltpu.SMEM)


def basis_call(kernel, group_index, inputs, order, out_shapes, extra, vmem, name):
    square = pltpu.VMEM((order, order), BF16)
    return pl.pallas_call(
        kernel,
        out_shape=tuple(jax.ShapeDtypeStruct(shape, BF16) for shape in out_shapes),
        in_specs=[SMEM] + [VMEM] * len(inputs),
        out_specs=(VMEM,) * len(out_shapes),
        scratch_shapes=[square, square, square, pltpu.VMEM((order, order), F32)]
        + extra
        + [
            pltpu.VMEM((TILE, TILE), F32),
            pltpu.VMEM((TILE, order), F32),
            pltpu.VMEM((order, TILE), F32),
        ],
        compiler_params=pltpu.CompilerParams(vmem_limit_bytes=vmem * 2**20),
        cost_estimate=pl.CostEstimate(
            flops=5 * 10**7 * order, bytes_accessed=10 * order**2, transcendentals=0
        ),
        name=name,
    )(group_index, *inputs)


def left_call(group_index, pieces):
    order = pieces[3].shape[0]
    shapes = [(order, order)] * 2
    return basis_call(left_kernel, group_index, pieces, order, shapes, [], 40, "left_basis")


def right_call(group_index, pieces, mixer):
    rows = mixer.shape[0]
    order, width = pieces[3].shape
    order -= rows // 2
    return basis_call(
        right_kernel,
        group_index,
        (*pieces, mixer),
        order,
        [(order, width), (rows, width)],
        [pltpu.VMEM((rows, order), BF16)],
        56,
        "right_basis",
    )


def pack_kernel(places, blocks, row_extent, col_extent, factor_r, factor_l, basis_r, basis_l, moment, out):
    rows_r, cols_r = factor_r.shape[1:]
    rows_l, cols_l = factor_l.shape[1:]

    def ids(rows, cols):
        return (
            lax.broadcasted_iota(jnp.int32, (rows, cols), 0) + places[0] * rows,
            lax.broadcasted_iota(jnp.int32, (rows, cols), 1) + places[1] * cols,
        )

    row_r, col_r = ids(rows_r, cols_r)
    row_l, col_l = ids(rows_l, cols_l)
    unit_r = (row_r == col_r).astype(F32)
    unit_l = (row_l == col_l).astype(F32)
    most_r = jnp.maximum(row_r, col_r)
    most_l = jnp.maximum(row_l, col_l)

    def step(r, carry):
        b = jnp.clip(blocks[r], 0, factor_r.shape[0] - 1)
        masked = jnp.where(most_r < col_extent[b], factor_r[b].astype(F32), unit_r)
        out[r, :rows_r, :] = masked.astype(BF16)
        out[r, rows_r : 2 * rows_r, :] = basis_r[b].astype(BF16)
        masked = jnp.where(most_l < row_extent[b], factor_l[b].astype(F32), unit_l)
        left = jnp.concatenate([masked, basis_l[b]], axis=1)
        both = jnp.concatenate([left, moment[b].astype(F32)], axis=0)
        out[r, 2 * rows_r :, :] = both.astype(BF16)
        return carry

    lax.fori_loop(0, out.shape[0], step, 0)


def packed(places, blocks, row_extent, col_extent, *arrays):
    rows_r, cols_r = arrays[0].shape[1:]
    rows_l = arrays[1].shape[1]
    return pl.pallas_call(
        pack_kernel,
        out_shape=jax.ShapeDtypeStruct(
            (blocks.shape[0], 2 * rows_r + 2 * rows_l, cols_r), BF16
        ),
        in_specs=[SMEM] * 4 + [VMEM] * 5,
        out_specs=VMEM,
        compiler_params=pltpu.CompilerParams(vmem_limit_bytes=56 * 2**20),
        cost_estimate=pl.CostEstimate(flops=10**9, bytes_accessed=4 * 2**20, transcendentals=0),
        name="packed",
    )(places, blocks, row_extent, col_extent, *arrays)


def shifted(piece, shift):
    count = lax.axis_size("grp")
    return lax.ppermute(piece, "grp", [(i, (i + shift) % count) for i in range(count)])


def near(piece):
    return shifted(piece, 1), shifted(piece, -1)


def gathered(piece, previous, following):
    half = piece.shape[0] // 2
    return piece, following, previous, shifted(previous[:half], 1), shifted(following[half:], -1)


def eye_piece(row_count, col_count, col_start):
    row_ids = lax.broadcasted_iota(jnp.int32, (row_count, col_count), 0)
    col_ids = lax.broadcasted_iota(jnp.int32, (row_count, col_count), 1) + col_start
    return (row_ids == col_ids).astype(F32)


def placement(owner, owner_count):
    block_ids = jnp.arange(owner.shape[0], dtype=jnp.int32)
    rows = jnp.arange(owner_count, dtype=jnp.int32)

    def total(hits, values):
        return jnp.sum(jnp.where(hits, values, 0), axis=1)

    earlier = (owner[:, None] == owner[None, :]) & (block_ids[None, :] < block_ids[:, None])
    repeated = jnp.any(earlier, axis=1)
    owned = rows[:, None] == owner[None, :]
    first_hits = owned & ~repeated[None, :]
    second_hits = owned & repeated[None, :]
    has_first = jnp.any(first_hits, axis=1)
    has_second = jnp.any(second_hits, axis=1)
    before = rows[None, :] < rows[:, None]
    empty_rank = total(before & ~has_first[None, :], 1)
    double_rank = total(before & has_second[None, :], 1)
    matched = ~has_first[:, None] & has_second[None, :] & (empty_rank[:, None] == double_rank[None, :])
    second_of = total(second_hits, block_ids[None, :])
    row_block = total(first_hits, block_ids[None, :]) + total(matched, second_of[None, :])
    second_row = jnp.sum(jnp.where(matched, rows[:, None], 0), axis=0)
    row_of = total(block_ids[:, None] == row_block[None, :], rows[None, :])
    return (row_block, row_of, second_row, has_first, has_second)


def pick(values, indices):
    return jnp.take(values, indices, axis=0, mode="clip")


def swap(pieces):
    return lax.all_to_all(pieces, "fsdp", split_axis=0, concat_axis=0, tiled=True)


def per_device(
    right_factor, left_factor, right_basis, left_basis, moment, owner, row_extent, col_extent
):
    owner_count = lax.axis_size("fsdp")
    fsdp_index = lax.axis_index("fsdp")
    group_index = lax.axis_index("grp")
    right_rows, right_cols = right_factor.shape[1:]
    left_rows, left_cols = left_factor.shape[1:]
    order_r = right_rows * owner_count
    order_l = left_rows * owner_count
    row_block, row_of, second_row, has_first, has_second = placement(owner, owner_count)
    group = group_index.astype(jnp.int32)[None]
    places = jnp.stack([fsdp_index, group_index]).astype(jnp.int32)
    pack = packed(
        places,
        row_block,
        row_extent,
        col_extent,
        right_factor,
        left_factor,
        right_basis,
        left_basis,
        moment,
    )
    pack = swap(pack)
    bounds = (0, right_rows, 2 * right_rows, 2 * right_rows + left_rows, 2 * (right_rows + left_rows))
    factor_r, basis_r, left_pair, moment_in = (
        pack[:, start:stop].reshape(-1, right_cols) for start, stop in zip(bounds, bounds[1:])
    )
    left_piece = jnp.concatenate([left_pair[:, :left_cols], left_pair[:, left_cols:]], axis=0)
    half = order_l // 2
    right_piece = jnp.concatenate([factor_r, moment_in[:half], basis_r, moment_in[half:]], axis=0)

    left_near, right_piece = lax.optimization_barrier((near(left_piece), right_piece))
    left_pieces = gathered(left_piece, *left_near)
    right_near = near(right_piece)
    fresh_l, mixer = left_call(group, left_pieces)
    fresh_l, right_near = lax.optimization_barrier((fresh_l, right_near))
    left_new = lax.dynamic_slice_in_dim(fresh_l, group_index * left_cols, left_cols, 1)
    rows_l = swap(left_new.reshape(owner_count, left_rows, left_cols))
    right_pieces = gathered(right_piece, *right_near)
    fresh_r, moment_out = right_call(group, right_pieces, mixer)
    fresh_r, rows_l = lax.optimization_barrier((fresh_r, rows_l))

    by_row = fresh_r.reshape(owner_count, MOST, left_rows, right_cols)
    back = jnp.concatenate(
        [
            by_row[:, 0],
            by_row[:, 1],
            moment_out.reshape(owner_count, left_rows, right_cols),
            pick(rows_l, second_row),
        ],
        axis=2,
    )
    back = swap(back)
    wide = MOST * right_cols
    second_r = swap(pick(back[:, :, :wide], second_row))
    second_r = jnp.stack([second_r[:, :, :right_cols], second_r[:, :, right_cols:]], axis=1)
    second_r = second_r.reshape(order_r, right_cols)
    second_l = back[:, :, wide + right_cols :].reshape(order_l, left_cols)
    new_moment = pick(back[:, :, wide : wide + right_cols], row_of)

    def slots(own, second):
        order, width = own.shape
        unit = eye_piece(order, width, group_index * width)
        filled = jnp.stack(
            [
                lax.dynamic_index_in_dim(has, fsdp_index, keepdims=False)
                for has in (has_first, has_second)
            ]
        )
        pair = jnp.stack([own, second]).astype(F32)
        return jnp.where(filled[:, None, None], pair, unit)[None]

    return (slots(fresh_r, second_r), slots(left_new, second_l), new_moment)


def solution(mesh):
    return jax.shard_map(
        per_device,
        mesh=mesh,
        in_specs=(
            P(None, "fsdp", "grp"),
            P(None, "fsdp", "grp"),
            P(None, "fsdp", "grp"),
            P(None, "fsdp", "grp"),
            P(None, "fsdp", "grp"),
            P(),
            P(),
            P(),
        ),
        out_specs=(
            P("fsdp", None, None, "grp"),
            P("fsdp", None, None, "grp"),
            P(None, "fsdp", "grp"),
        ),
        check_vma=False,
    )
```
